32 devices in a mesh: groups: 2 (over y), chol: 4 (over z), walk: 2 (over x), kpt: 2 (over core).
Axes of the slice: x: 2, y: 2, z: 4, core: 2. Of those that a mesh axis runs over, the one named last changes fastest.
Arguments:
- green_blocks: bfloat16 [16, 4, 64, 1024], P(('groups', 'chol', 'walk'), None, 'kpt'), parts along dimension 0, may hold values from -6 to 6
- chol_vectors: bfloat16 [4, 64, 1024, 256], P('chol', 'kpt', 'walk'), may hold values from -0.0234375 to 0.0234375
- aux_fields: float32 [16, 4, 256], P('groups', 'chol'), parts along dimension 0, may hold values from -6 to 6
- orbitals: bfloat16 [16, 64, 768], P(('groups', 'chol', 'walk'), 'kpt'), parts along dimension 0, may hold values from -6 to 6
- transfer_table: int32 [64, 4], replicated, may hold values from 0 to 63, as said below
Outputs:
- force_bias: float32 [16, 4, 256], P('groups', 'chol'), parts along dimension 0
- new_orbitals: bfloat16 [16, 64, 768], P(('groups', 'chol', 'walk'), 'kpt'), parts along dimension 0
The draws below stay inside these ranges and needn't reach their ends.
There are 2 independent parts, one for each index of `groups`. The reference program is written for one: setup_inputs(seed, part) draws one part's arguments, and reference() takes and returns one part's arrays. A program takes and returns all parts, laid end to end along the dimension named above; an argument that names none is the same for every part. Nothing has to cross between parts.
Inputs may be any that keep to these rules, and one draw needn't show every extreme that they name: `transfer_table`: column j holds, for every k-point k = 4**2 kx + 4 ky + kz of the 4 x 4 x 4 grid, the index of k - q_j taken modulo the grid in each component, for 4 distinct transfers q_j; each column is a permutation of the k-points.
All inputs are finite; a program needn't handle non-finite values.
Results may differ from the reference program's by a relative error of at most 0.022.
Values may be sent and summed in bfloat16 or wider, within the bound.
A program may use at most 64 MiB of HBM per device.

```python
import jax
import jax.numpy as jnp
from jax import lax

NORB = 32
SPOCC = 24
NCHOL = 256
KGRID = 4
TAYLOR = 4
K = 64
PAIRS = 1024
QW = 4
W = 8


def draw_transfer_table(key, part):
    key = jax.random.fold_in(key, 7)
    chosen = jax.random.permutation(key, K)[:QW]
    kpoint = jnp.arange(K, dtype=jnp.int32)
    first = kpoint // (KGRID * KGRID)
    second = kpoint // KGRID % KGRID
    third = kpoint % KGRID
    qfirst = chosen // (KGRID * KGRID)
    qsecond = chosen // KGRID % KGRID
    qthird = chosen % KGRID
    dfirst = (first[:, None] - qfirst[None, :]) % KGRID
    dsecond = (second[:, None] - qsecond[None, :]) % KGRID
    dthird = (third[:, None] - qthird[None, :]) % KGRID
    return (dfirst * KGRID * KGRID + dsecond * KGRID + dthird).astype(jnp.int32)


def steps_of(rng, extent, pieces, smallest, largest):
    def one(dim, parts):
        heights = jax.random.uniform(jax.random.fold_in(jax.random.fold_in(rng, 6), dim), (parts,), jnp.float32, smallest / len(pieces), largest / len(pieces))
        return jnp.repeat(jnp.exp(heights), extent[dim] // parts).reshape((-1,) + (1,) * (len(extent) - dim - 1))

    gain = one(*pieces[0])
    for cut in pieces[1:]:
        gain = gain * one(*cut)
    return gain


def gaussian(key, shape, width, reach, pieces=(), kind=jnp.bfloat16):
    entries = width * jax.random.normal(key, shape, jnp.float32)
    if pieces:
        entries = entries * steps_of(key, shape, pieces, -0.22, 0.18)
    return jnp.clip(entries, -reach, reach).astype(kind)


def setup_inputs(seed: int = 0, part: int = 0) -> dict:
    key_of = jax.random.split(jax.random.key(seed), 6)
    part_keys = jax.random.split(jax.random.fold_in(key_of[5], part), 6)
    green_blocks = gaussian(part_keys[0], (W, QW, K, PAIRS), 1.0, 6.0, ((0, 8), (2, 2)))
    chol_vectors = gaussian(key_of[1], (QW, K, PAIRS, NCHOL), (K * PAIRS) ** -0.5, 0.0234375, ((0, 4), (1, 2), (2, 2)))
    aux_fields = gaussian(part_keys[2], (W, QW, NCHOL), 1.0, 6.0, ((1, 4),), jnp.float32)
    orbitals = gaussian(part_keys[3], (W, K, NORB * SPOCC), 1.0, 6.0, ((0, 8), (1, 2)))
    transfer_table = draw_transfer_table(jax.random.fold_in(key_of[5], 71), part)
    return {"green_blocks": green_blocks, "chol_vectors": chol_vectors, "aux_fields": aux_fields, "orbitals": orbitals, "transfer_table": transfer_table}


bias_scale = 0.5


def reference(green_blocks, chol_vectors, aux_fields, orbitals, transfer_table):
    walkers = green_blocks.shape[0]
    kpoints = green_blocks.shape[2]
    pair_count = green_blocks.shape[3]
    channels = chol_vectors.shape[3]

    def one_transfer(transfer):
        green_rows = lax.dynamic_index_in_dim(green_blocks, transfer, 1, keepdims=False).reshape(walkers, kpoints * pair_count)
        vectors = lax.dynamic_index_in_dim(chol_vectors, transfer, 0, keepdims=False).reshape(kpoints * pair_count, channels)
        bias_rows = jnp.dot(green_rows, vectors, preferred_element_type=jnp.float32)
        field_row = lax.dynamic_index_in_dim(aux_fields, transfer, 1, keepdims=False)
        shifted = (field_row - jnp.clip(-bias_scale * bias_rows, -1.0, 1.0)).astype(jnp.bfloat16)
        operator_rows = jnp.dot(shifted, vectors.T, preferred_element_type=jnp.float32).astype(jnp.bfloat16)
        return bias_rows, operator_rows

    biases, operators = lax.map(one_transfer, jnp.arange(QW, dtype=jnp.int32))
    force_bias = jnp.transpose(biases, (1, 0, 2))

    series_term = orbitals.reshape(walkers, kpoints, NORB, SPOCC)
    summed = series_term.astype(jnp.float32)
    for degree in range(1, TAYLOR + 1):
        def add_transfer(running, transfer, current=series_term):
            operator_block = lax.dynamic_index_in_dim(operators, transfer, 0, keepdims=False)
            operator_block = operator_block.reshape(walkers, kpoints, NORB, NORB).astype(jnp.float32)
            column = lax.dynamic_index_in_dim(transfer_table, transfer, 1, keepdims=False)
            source = jnp.take(current, column, axis=1).astype(jnp.float32)
            return running + jnp.einsum("wkij,wkjc->wkic", operator_block, source), None

        start = jnp.zeros((walkers, kpoints, NORB, SPOCC), jnp.float32)
        accumulated, _ = lax.scan(add_transfer, start, jnp.arange(QW, dtype=jnp.int32))
        update = accumulated / degree
        summed = summed + update
        series_term = update.astype(jnp.bfloat16)
    new_orbitals = summed.reshape(walkers, kpoints, NORB * SPOCC).astype(jnp.bfloat16)
    return force_bias, new_orbitals
```

```python
import functools

import jax
import jax.numpy as jnp
from jax import lax
from jax.experimental import pallas as pl
from jax.experimental.pallas import tpu as pltpu
from jax.sharding import PartitionSpec as P

NORB = 32
SPOCC = 24
TAYLOR = 4
LANES = 128
HALF = 16
MESH = pl.DeviceIdType.MESH


bias_scale = 0.5


def repeat(count, body):
    if count <= 16:
        for step in range(count):
            body(step)
    else:
        lax.fori_loop(0, count, lambda step, carry: (body(step), carry)[1], 0)


def kernel(
    sizes,
    table_ref,
    green_ref,
    chol_ref,
    aux_ref,
    orb_ref,
    bias_out,
    orb_out,
    chol_v,
    arrived,
    parts,
    aux_v,
    bias_v,
    op_send,
    ops,
    relay,
    blocks,
    orb_v,
    total,
    term0,
    term1,
    term2,
    term3,
    chol_sem,
    small_sem,
    own_sem,
    green_send,
    green_recv,
    part_send,
    part_recv,
    op_sendsem,
    op_recv,
    term_send,
    term_recv,
):
    C, H, KD, PD, N = sizes
    W = C * H
    halves = KD // HALF
    my_c, my_h, my_k = lax.axis_index("chol"), lax.axis_index("walk"), lax.axis_index("kpt")
    me = my_c * H + my_h
    terms = (term0, term1, term2, term3)
    quads = C // 4
    chol_chunks = chol_sem.shape[0]
    chunk_k = KD // chol_chunks

    orb_copy = pltpu.make_async_copy(orb_ref.at[0], orb_v, small_sem.at[0])
    orb_copy.start()
    aux_copy = pltpu.make_async_copy(aux_ref, aux_v, small_sem.at[1])
    aux_copy.start()

    def chol_copy(chunk):
        rows = pl.ds(chunk * chunk_k, chunk_k)
        return pltpu.make_async_copy(chol_ref.at[0, rows], chol_v.at[rows], chol_sem.at[chunk])

    def own_green(half):
        rows = pl.ds(half * HALF, HALF)
        slab = pl.ds(pl.multiple_of(my_h * PD, PD), PD)
        return pltpu.make_async_copy(
            green_ref.at[0, my_c, rows, slab], arrived.at[me, rows], own_sem.at[half]
        )

    barrier = pltpu.get_barrier_semaphore()

    def greet(step):
        peer = lax.rem(me + 1 + step, W)
        pl.semaphore_signal(
            barrier, inc=1, device_id={"chol": peer // H, "walk": lax.rem(peer, H)}, device_id_type=MESH
        )

    repeat(W - 1, greet)

    def greet_other(step):
        pl.semaphore_signal(
            barrier, inc=1, device_id={"walk": step, "kpt": 1 - my_k}, device_id_type=MESH
        )

    repeat(H, greet_other)
    for half in range(halves):
        own_green(half).start()
    pl.semaphore_wait(barrier, W - 1 + H)

    def green_copy(half, step):
        peer = lax.rem(me + 1 + step, W)
        pc, ph = peer // H, lax.rem(peer, H)
        rows = pl.ds(half * HALF, HALF)
        slab = pl.ds(pl.multiple_of(ph * PD, PD), PD)
        return pltpu.make_async_remote_copy(
            src_ref=green_ref.at[0, pc, rows, slab],
            dst_ref=arrived.at[me, rows],
            send_sem=green_send.at[half, step],
            recv_sem=green_recv.at[half, me],
            device_id={"chol": pc, "walk": ph},
            device_id_type=MESH,
        )

    def green_wait(half, step):
        peer = lax.rem(me + 1 + step, W)
        pc, ph = peer // H, lax.rem(peer, H)
        rows = pl.ds(half * HALF, HALF)
        pltpu.make_async_remote_copy(
            src_ref=arrived.at[peer, rows],
            dst_ref=arrived.at[peer, rows],
            send_sem=green_send.at[half, step],
            recv_sem=green_recv.at[half, peer],
            device_id={"chol": pc, "walk": ph},
            device_id_type=MESH,
        ).wait_recv()

    for half in range(halves):
        repeat(W - 1, lambda step: green_copy(half, step).start())
    for chunk in range(chol_chunks):
        chol_copy(chunk).start()

    lane = lax.broadcasted_iota(jnp.int32, (KD, LANES), 1)
    orb_copy.wait()
    for l in range(NORB):
        v, off = divmod(l * SPOCC, LANES)
        shift = (LANES - off) % LANES
        piece = orb_v[:, v * LANES : (v + 1) * LANES].astype(jnp.float32)
        if shift:
            piece = pltpu.roll(piece, shift, 1)
        if off + SPOCC > LANES:
            following = orb_v[:, (v + 1) * LANES : (v + 2) * LANES].astype(jnp.float32)
            piece = jnp.where(lane < LANES - off, piece, pltpu.roll(following, shift, 1))
        relay[l * KD : (l + 1) * KD, :] = jnp.where(lane < SPOCC, piece, 0.0)
    for k in range(KD):
        rows = relay[pl.ds(k, NORB, stride=KD), :]
        total[k] = rows
        term0[my_k * KD + k] = rows.astype(jnp.bfloat16)

    chunks = 4
    per_chunk = KD // chunks

    def term_copy(degree, chunk):
        rows = pl.ds(my_k * KD + chunk * per_chunk, per_chunk)
        return pltpu.make_async_remote_copy(
            src_ref=terms[degree].at[rows],
            dst_ref=terms[degree].at[rows],
            send_sem=term_send.at[degree, chunk],
            recv_sem=term_recv.at[degree, chunk],
            device_id={"kpt": 1 - my_k},
            device_id_type=MESH,
        )

    def term_wait(degree, chunk):
        rows = pl.ds((1 - my_k) * KD + chunk * per_chunk, per_chunk)
        pltpu.make_async_remote_copy(
            src_ref=terms[degree].at[rows],
            dst_ref=terms[degree].at[rows],
            send_sem=term_send.at[degree, chunk],
            recv_sem=term_recv.at[degree, chunk],
            device_id={"kpt": 1 - my_k},
            device_id_type=MESH,
        ).wait_recv()

    for chunk in range(chunks):
        term_copy(0, chunk).start()

    partial = jnp.zeros((W, N), jnp.float32)
    for half in range(halves):
        own_green(half).wait()
        repeat(W - 1, lambda step: green_wait(half, step))
        k0 = half * HALF
        for chunk in range(chol_chunks // halves):
            chol_copy(half * (chol_chunks // halves) + chunk).wait()
        for group in range(0, HALF, 8):
            rows = arrived[:, k0 : k0 + HALF, :].astype(jnp.float32)[:, group : group + 8, :]
            rows = jnp.swapaxes(rows, 0, 1)
            left = jnp.concatenate([rows[k] for k in range(8)], axis=1).astype(jnp.bfloat16)
            right = chol_v[k0 + group : k0 + group + 8].reshape(8 * PD, N)
            partial += jnp.dot(left, right, preferred_element_type=jnp.float32)

    slot = my_h * 2 + my_k
    parts[slot] = partial

    def part_copy(step):
        peer = lax.rem(slot + 1 + step, 2 * H)
        return pltpu.make_async_remote_copy(
            src_ref=parts.at[slot],
            dst_ref=parts.at[slot],
            send_sem=part_send.at[step],
            recv_sem=part_recv.at[slot],
            device_id={"walk": peer // 2, "kpt": lax.rem(peer, 2)},
            device_id_type=MESH,
        )

    def part_wait(step):
        peer = lax.rem(slot + 1 + step, 2 * H)
        pltpu.make_async_remote_copy(
            src_ref=parts.at[peer],
            dst_ref=parts.at[peer],
            send_sem=part_send.at[step],
            recv_sem=part_recv.at[peer],
            device_id={"walk": peer // 2, "kpt": lax.rem(peer, 2)},
            device_id_type=MESH,
        ).wait_recv()

    repeat(2 * H - 1, lambda step: part_copy(step).start())
    aux_copy.wait()
    fields = aux_v[:, 0, :]
    repeat(2 * H - 1, part_wait)
    bias = parts[0]
    for other in range(1, 2 * H):
        bias += parts[other]
    shifted = (fields - jnp.clip(-bias_scale * bias, -1.0, 1.0)).astype(jnp.bfloat16)

    def op_copy(half, step):
        peer = lax.rem(me + 1 + step, W)
        pc, ph = peer // H, lax.rem(peer, H)
        rows = pl.ds(half * HALF, HALF)
        slab = pl.ds(pl.multiple_of(my_h * PD, PD), PD)
        return pltpu.make_async_remote_copy(
            src_ref=op_send.at[peer, rows],
            dst_ref=ops.at[my_c, rows, slab],
            send_sem=op_sendsem.at[half, step],
            recv_sem=op_recv.at[half, me],
            device_id={"chol": pc, "walk": ph},
            device_id_type=MESH,
        )

    def op_wait(half, step):
        peer = lax.rem(me + 1 + step, W)
        pc, ph = peer // H, lax.rem(peer, H)
        rows = pl.ds(half * HALF, HALF)
        slab = pl.ds(pl.multiple_of(ph * PD, PD), PD)
        pltpu.make_async_remote_copy(
            src_ref=op_send.at[peer, rows],
            dst_ref=ops.at[pc, rows, slab],
            send_sem=op_sendsem.at[half, step],
            recv_sem=op_recv.at[half, peer],
            device_id={"chol": pc, "walk": ph},
            device_id_type=MESH,
        ).wait_recv()

    def own_op(half):
        rows = pl.ds(half * HALF, HALF)
        slab = pl.ds(pl.multiple_of(my_h * PD, PD), PD)
        return pltpu.make_async_copy(
            op_send.at[me, rows], ops.at[my_c, rows, slab], own_sem.at[half]
        )

    for half in range(halves):
        k0 = half * HALF
        pieces = []
        for group in range(0, HALF, 8):
            right = chol_v[k0 + group : k0 + group + 8].reshape(8 * PD, N)
            out = lax.dot_general(
                shifted, right, (((1,), (1,)), ((), ())), preferred_element_type=jnp.float32
            )
            stacked = jnp.stack([out[:, k * PD : (k + 1) * PD] for k in range(8)], axis=0)
            pieces.append(jnp.swapaxes(stacked, 0, 1))
        op_send[:, k0 : k0 + HALF, :] = jnp.concatenate(pieces, axis=1).astype(jnp.bfloat16)
        repeat(W - 1, lambda step: op_copy(half, step).start())
        own_op(half).start()

    bias_v[:, 0, :] = bias
    bias_copy = pltpu.make_async_copy(bias_v, bias_out, small_sem.at[1])
    bias_copy.start()

    narrow = lax.broadcasted_iota(jnp.int32, (HALF, LANES), 1) // NORB
    for half in range(halves):
        k0 = half * HALF
        own_op(half).wait()
        repeat(W - 1, lambda step: op_wait(half, step))
        for quad in range(quads):
            for tile in range(NORB * NORB // LANES):
                given = [
                    ops[4 * quad + j, k0 : k0 + HALF, tile * LANES : (tile + 1) * LANES].astype(jnp.float32)
                    for j in range(4)
                ]
                for inner in range(4):
                    made = None
                    for j in range(4):
                        turn = (j - inner) % 4 * NORB
                        value = pltpu.roll(given[j], turn, 1) if turn else given[j]
                        made = value if made is None else jnp.where(narrow == j, value, made)
                    row = (tile * 4 + inner) * HALF
                    relay[row : row + HALF, :] = made
            for k in range(HALF):
                rows = relay[pl.ds(k, NORB, stride=HALF), :]
                blocks[k0 + k, :, quad * LANES : (quad + 1) * LANES] = rows.astype(jnp.bfloat16)

    for degree in range(1, TAYLOR + 1):
        source = terms[degree - 1]
        for chunk in range(chunks):
            term_wait(degree - 1, chunk)
        for chunk in range(chunks):
            for inner in range(per_chunk):
                k = chunk * per_chunk + inner
                right = jnp.concatenate(
                    [source[table_ref[my_k * KD + k, j]] for j in range(C)], axis=0
                )
                update = jnp.dot(blocks[k], right, preferred_element_type=jnp.float32)
                if degree > 1:
                    update = update * (1.0 / degree)
                total[k] += update
                if degree < TAYLOR:
                    terms[degree][my_k * KD + k] = update.astype(jnp.bfloat16)
            if degree < TAYLOR:
                term_copy(degree, chunk).start()

    made = [jnp.zeros((KD, LANES), jnp.float32) for _ in range(NORB * SPOCC // LANES)]
    flat = total.reshape(KD * NORB, LANES)
    for i in range(NORB):
        v, off = divmod(i * SPOCC, LANES)
        rows = flat[pl.ds(i, KD, stride=NORB), :]
        if off:
            rows = pltpu.roll(rows, off, 1)
        if off + SPOCC > LANES:
            made[v] += jnp.where(lane >= off, rows, 0.0)
            made[v + 1] += jnp.where(lane < off, rows, 0.0)
        else:
            made[v] += rows
    orb_v[...] = jnp.concatenate(made, axis=1).astype(jnp.bfloat16)
    result = pltpu.make_async_copy(orb_v, orb_out.at[0], small_sem.at[0])
    result.start()

    for half in range(halves):
        repeat(W - 1, lambda step: green_copy(half, step).wait_send())
        repeat(W - 1, lambda step: op_copy(half, step).wait_send())
    repeat(2 * H - 1, lambda step: part_copy(step).wait_send())
    for degree in range(TAYLOR):
        for chunk in range(chunks):
            term_copy(degree, chunk).wait_send()
    bias_copy.wait()
    result.wait()


def per_device(green_blocks, chol_vectors, aux_fields, orbitals, transfer_table):
    C = lax.axis_size("chol")
    H = lax.axis_size("walk")
    KD = green_blocks.shape[2]
    PD = chol_vectors.shape[2]
    N = chol_vectors.shape[3]
    K = transfer_table.shape[0]
    W = C * H
    anywhere = pl.BlockSpec(memory_space=pl.ANY)
    halves = KD // HALF
    chol_chunks = 4
    term = pltpu.VMEM((K, NORB, LANES), jnp.bfloat16)
    dma = pltpu.SemaphoreType.DMA
    return pl.pallas_call(
        functools.partial(kernel, (C, H, KD, PD, N)),
        out_shape=(
            jax.ShapeDtypeStruct(aux_fields.shape, jnp.float32),
            jax.ShapeDtypeStruct(orbitals.shape, jnp.bfloat16),
        ),
        in_specs=[pl.BlockSpec(memory_space=pltpu.SMEM)] + [anywhere] * 4,
        out_specs=(anywhere, anywhere),
        scratch_shapes=[
            pltpu.VMEM((KD, PD, N), jnp.bfloat16),
            pltpu.VMEM((W, KD, PD), jnp.bfloat16),
            pltpu.VMEM((2 * H, W, N), jnp.float32),
            pltpu.VMEM((W, 1, N), jnp.float32),
            pltpu.VMEM((W, 1, N), jnp.float32),
            pltpu.VMEM((W, KD, PD), jnp.bfloat16),
            pltpu.VMEM((C, KD, NORB * NORB), jnp.bfloat16),
            pltpu.VMEM((NORB * KD, LANES), jnp.float32),
            pltpu.VMEM((KD, NORB, C * NORB), jnp.bfloat16),
            pltpu.VMEM((KD, NORB * SPOCC), jnp.bfloat16),
            pltpu.VMEM((KD, NORB, LANES), jnp.float32),
            term,
            term,
            term,
            term,
            dma((chol_chunks,)),
            dma((2,)),
            dma((halves,)),
            dma((halves, W)),
            dma((halves, W)),
            dma((2 * H,)),
            dma((2 * H,)),
            dma((halves, W)),
            dma((halves, W)),
            dma((TAYLOR, 4)),
            dma((TAYLOR, 4)),
        ],
        compiler_params=pltpu.CompilerParams(
            collective_id=0, has_side_effects=True, vmem_limit_bytes=48 * 1024 * 1024
        ),
        name="walker_step",
    )(transfer_table, green_blocks, chol_vectors, aux_fields, orbitals)


def solution(mesh):
    placed = (
        P(("groups", "chol", "walk"), None, "kpt", None),
        P("chol", "kpt", "walk", None),
        P("groups", "chol", None),
        P(("groups", "chol", "walk"), "kpt", None),
        P(),
    )
    return jax.shard_map(
        per_device,
        mesh=mesh,
        in_specs=placed,
        out_specs=(P("groups", "chol", None), P(("groups", "chol", "walk"), "kpt", None)),
        check_vma=False,
    )
```

```python
import functools

import jax
import jax.numpy as jnp
from jax import lax
from jax.experimental import pallas as pl
from jax.experimental.pallas import tpu as pltpu
from jax.sharding import PartitionSpec as P

NORB = 32
SPOCC = 24
TAYLOR = 4
LANES = 128
HALF = 16
MESH = pl.DeviceIdType.MESH


bias_scale = 0.5


def repeat(count, body):
    if count <= 16:
        for step in range(count):
            body(step)
    else:
        lax.fori_loop(0, count, lambda step, carry: (body(step), carry)[1], 0)


def kernel(
    sizes,
    table_in,
    green_ref,
    chol_ref,
    aux_ref,
    orb_ref,
    bias_out,
    orb_out,
    chol_v,
    arrived,
    parts,
    aux_v,
    op_send,
    ops,
    relay,
    blocks,
    orb_v,
    total,
    term0,
    term1,
    term2,
    term3,
    table_ref,
    chol_sem,
    small_sem,
    own_sem,
    green_send,
    green_recv,
    part_send,
    part_recv,
    op_sendsem,
    op_recv,
    term_send,
    term_recv,
):
    C, H, KD, PD, N = sizes
    W = C * H
    halves = KD // HALF
    splits = green_send.shape[0] // halves
    pieces = halves * splits
    width = PD // splits
    my_c, my_h, my_k = lax.axis_index("chol"), lax.axis_index("walk"), lax.axis_index("kpt")
    me = my_c * H + my_h
    terms = (term0, term1, term2, term3)
    quads = C // 4
    chol_chunks = chol_sem.shape[0]
    chunk_k = KD // chol_chunks

    top, low = my_c // (C // 2), lax.rem(my_c, C // 2)

    def peer_at(step):
        near = step // (W // 2)
        rest = step % (W // 2) + near
        pc = lax.rem(top + 1 - near, 2) * (C // 2) + lax.rem(low + rest // H, C // 2)
        ph = lax.rem(my_h + rest % H, H)
        return pc, ph, pc * H + ph

    def rows_of(piece):
        return pl.ds(piece // splits * HALF, HALF)

    def slab_of(h, piece):
        start = h * PD + piece % splits * width
        return pl.ds(pl.multiple_of(start, LANES), width)

    def part_of(piece):
        return pl.ds(piece % splits * width, width)

    barrier = pltpu.get_barrier_semaphore()

    def greet(step):
        pc, ph, _ = peer_at(step)
        pl.semaphore_signal(barrier, inc=1, device_id={"chol": pc, "walk": ph}, device_id_type=MESH)

    repeat(W - 1, greet)

    def greet_other(step):
        pl.semaphore_signal(
            barrier, inc=1, device_id={"walk": step, "kpt": 1 - my_k}, device_id_type=MESH
        )

    repeat(H, greet_other)
    orb_copy = pltpu.make_async_copy(orb_ref.at[0], orb_v, small_sem.at[0])
    orb_copy.start()
    aux_copy = pltpu.make_async_copy(aux_ref, aux_v, small_sem.at[1])
    aux_copy.start()
    table_copy = pltpu.make_async_copy(table_in, table_ref, small_sem.at[2])
    table_copy.start()

    def chol_copy(chunk):
        rows = pl.ds(chunk * chunk_k, chunk_k)
        return pltpu.make_async_copy(chol_ref.at[0, rows], chol_v.at[rows], chol_sem.at[chunk])

    def own_green(piece):
        rows = rows_of(piece)
        return pltpu.make_async_copy(
            green_ref.at[0, my_c, rows, slab_of(my_h, piece)],
            arrived.at[me, rows, part_of(piece)],
            own_sem.at[piece],
        )

    for piece in range(pieces):
        own_green(piece).start()
    pl.semaphore_wait(barrier, W - 1 + H)

    def green_copy(piece, step):
        pc, ph, _ = peer_at(step)
        rows = rows_of(piece)
        return pltpu.make_async_remote_copy(
            src_ref=green_ref.at[0, pc, rows, slab_of(ph, piece)],
            dst_ref=arrived.at[me, rows, part_of(piece)],
            send_sem=green_send.at[piece, step],
            recv_sem=green_recv.at[piece, me],
            device_id={"chol": pc, "walk": ph},
            device_id_type=MESH,
        )

    def green_wait(piece, step):
        pc, ph, peer = peer_at(step)
        landed = arrived.at[peer, rows_of(piece), part_of(piece)]
        pltpu.make_async_remote_copy(
            src_ref=landed,
            dst_ref=landed,
            send_sem=green_send.at[piece, step],
            recv_sem=green_recv.at[piece, peer],
            device_id={"chol": pc, "walk": ph},
            device_id_type=MESH,
        ).wait_recv()

    for piece in range(pieces):
        repeat(W - 1, lambda step: green_copy(piece, step).start())
    for chunk in range(chol_chunks):
        chol_copy(chunk).start()

    lane = lax.broadcasted_iota(jnp.int32, (KD, LANES), 1)
    orb_copy.wait()
    for l in range(NORB):
        v, off = divmod(l * SPOCC, LANES)
        shift = (LANES - off) % LANES
        piece = orb_v[:, v * LANES : (v + 1) * LANES].astype(jnp.float32)
        if shift:
            piece = pltpu.roll(piece, shift, 1)
        if off + SPOCC > LANES:
            following = orb_v[:, (v + 1) * LANES : (v + 2) * LANES].astype(jnp.float32)
            piece = jnp.where(lane < LANES - off, piece, pltpu.roll(following, shift, 1))
        relay[l * KD : (l + 1) * KD, :] = jnp.where(lane < SPOCC, piece, 0.0)
    for k in range(KD):
        rows = relay[pl.ds(k, NORB, stride=KD), :]
        total[k] = rows
        term0[my_k * KD + k] = rows.astype(jnp.bfloat16)

    chunks = 4
    per_chunk = KD // chunks

    def term_copy(degree, chunk):
        rows = pl.ds(my_k * KD + chunk * per_chunk, per_chunk)
        return pltpu.make_async_remote_copy(
            src_ref=terms[degree].at[rows],
            dst_ref=terms[degree].at[rows],
            send_sem=term_send.at[degree, chunk],
            recv_sem=term_recv.at[degree, chunk],
            device_id={"kpt": 1 - my_k},
            device_id_type=MESH,
        )

    def term_wait(degree, chunk):
        rows = pl.ds((1 - my_k) * KD + chunk * per_chunk, per_chunk)
        pltpu.make_async_remote_copy(
            src_ref=terms[degree].at[rows],
            dst_ref=terms[degree].at[rows],
            send_sem=term_send.at[degree, chunk],
            recv_sem=term_recv.at[degree, chunk],
            device_id={"kpt": 1 - my_k},
            device_id_type=MESH,
        ).wait_recv()

    for chunk in range(chunks):
        term_copy(0, chunk).start()

    partial = jnp.zeros((W, N), jnp.float32)
    for piece in range(pieces):
        own_green(piece).wait()
        repeat(W - 1, lambda step: green_wait(piece, step))
        half, split = divmod(piece, splits)
        k0, p0 = half * HALF, split * width
        if split == 0:
            for chunk in range(chol_chunks // halves):
                chol_copy(half * (chol_chunks // halves) + chunk).wait()
        for group in range(0, HALF, 8):
            rows = arrived[:, k0 : k0 + HALF, p0 : p0 + width].astype(jnp.float32)
            rows = jnp.swapaxes(rows[:, group : group + 8, :], 0, 1)
            left = jnp.concatenate([rows[k] for k in range(8)], axis=1).astype(jnp.bfloat16)
            right = chol_v[k0 + group : k0 + group + 8, p0 : p0 + width].reshape(8 * width, N)
            partial += jnp.dot(left, right, preferred_element_type=jnp.float32)

    slot = my_h * 2 + my_k
    parts[slot] = partial

    def part_copy(step):
        peer = lax.rem(slot + 1 + step, 2 * H)
        return pltpu.make_async_remote_copy(
            src_ref=parts.at[slot],
            dst_ref=parts.at[slot],
            send_sem=part_send.at[step],
            recv_sem=part_recv.at[slot],
            device_id={"walk": peer // 2, "kpt": lax.rem(peer, 2)},
            device_id_type=MESH,
        )

    def part_wait(step):
        peer = lax.rem(slot + 1 + step, 2 * H)
        pltpu.make_async_remote_copy(
            src_ref=parts.at[peer],
            dst_ref=parts.at[peer],
            send_sem=part_send.at[step],
            recv_sem=part_recv.at[peer],
            device_id={"walk": peer // 2, "kpt": lax.rem(peer, 2)},
            device_id_type=MESH,
        ).wait_recv()

    repeat(2 * H - 1, lambda step: part_copy(step).start())
    aux_copy.wait()
    table_copy.wait()
    fields = aux_v[:, 0, :]
    repeat(2 * H - 1, part_wait)
    bias = parts[0]
    for other in range(1, 2 * H):
        bias += parts[other]
    shifted = (fields - jnp.clip(-bias_scale * bias, -1.0, 1.0)).astype(jnp.bfloat16)

    def op_copy(piece, step):
        pc, ph, peer = peer_at(step)
        rows = rows_of(piece)
        return pltpu.make_async_remote_copy(
            src_ref=op_send.at[peer, rows, part_of(piece)],
            dst_ref=ops.at[my_c, rows, slab_of(my_h, piece)],
            send_sem=op_sendsem.at[piece, step],
            recv_sem=op_recv.at[piece, me],
            device_id={"chol": pc, "walk": ph},
            device_id_type=MESH,
        )

    def op_wait(piece, step):
        pc, ph, peer = peer_at(step)
        rows = rows_of(piece)
        pltpu.make_async_remote_copy(
            src_ref=op_send.at[peer, rows, part_of(piece)],
            dst_ref=ops.at[pc, rows, slab_of(ph, piece)],
            send_sem=op_sendsem.at[piece, step],
            recv_sem=op_recv.at[piece, peer],
            device_id={"chol": pc, "walk": ph},
            device_id_type=MESH,
        ).wait_recv()

    def own_op(piece):
        rows = rows_of(piece)
        return pltpu.make_async_copy(
            op_send.at[me, rows, part_of(piece)],
            ops.at[my_c, rows, slab_of(my_h, piece)],
            own_sem.at[piece],
        )

    for piece in range(pieces):
        half, split = divmod(piece, splits)
        k0, p0 = half * HALF, split * width
        made = []
        for group in range(0, HALF, 8):
            right = chol_v[k0 + group : k0 + group + 8, p0 : p0 + width].reshape(8 * width, N)
            out = lax.dot_general(
                shifted, right, (((1,), (1,)), ((), ())), preferred_element_type=jnp.float32
            )
            stacked = jnp.stack([out[:, k * width : (k + 1) * width] for k in range(8)], axis=0)
            made.append(jnp.swapaxes(stacked, 0, 1))
        op_send[:, k0 : k0 + HALF, p0 : p0 + width] = jnp.concatenate(made, axis=1).astype(jnp.bfloat16)
        repeat(W - 1, lambda step: op_copy(piece, step).start())
        own_op(piece).start()

    bias_out[:, 0, :] = bias

    narrow = lax.broadcasted_iota(jnp.int32, (HALF, LANES), 1) // NORB
    for half in range(halves):
        k0 = half * HALF
        for piece in range(half * splits, (half + 1) * splits):
            own_op(piece).wait()
            repeat(W - 1, lambda step: op_wait(piece, step))
        for quad in range(quads):
            for tile in range(NORB * NORB // LANES):
                given = [
                    ops[4 * quad + j, k0 : k0 + HALF, tile * LANES : (tile + 1) * LANES].astype(jnp.float32)
                    for j in range(4)
                ]
                for inner in range(4):
                    made = None
                    for j in range(4):
                        turn = (j - inner) % 4 * NORB
                        value = pltpu.roll(given[j], turn, 1) if turn else given[j]
                        made = value if made is None else jnp.where(narrow == j, value, made)
                    row = (tile * 4 + inner) * HALF
                    relay[row : row + HALF, :] = made
            for k in range(HALF):
                rows = relay[pl.ds(k, NORB, stride=HALF), :]
                blocks[k0 + k, :, quad * LANES : (quad + 1) * LANES] = rows.astype(jnp.bfloat16)

    for degree in range(1, TAYLOR + 1):
        source = terms[degree - 1]
        for chunk in range(chunks):
            term_wait(degree - 1, chunk)
        for chunk in range(chunks):
            for inner in range(per_chunk):
                k = chunk * per_chunk + inner
                right = jnp.concatenate(
                    [source[table_ref[j, my_k * KD + k]] for j in range(C)], axis=0
                )
                update = jnp.dot(blocks[k], right, preferred_element_type=jnp.float32)
                if degree > 1:
                    update = update * (1.0 / degree)
                total[k] += update
                if degree < TAYLOR:
                    terms[degree][my_k * KD + k] = update.astype(jnp.bfloat16)
            if degree < TAYLOR:
                term_copy(degree, chunk).start()

    made = [jnp.zeros((KD, LANES), jnp.float32) for _ in range(NORB * SPOCC // LANES)]
    flat = total.reshape(KD * NORB, LANES)
    for i in range(NORB):
        v, off = divmod(i * SPOCC, LANES)
        rows = flat[pl.ds(i, KD, stride=NORB), :]
        if off:
            rows = pltpu.roll(rows, off, 1)
        if off + SPOCC > LANES:
            made[v] += jnp.where(lane >= off, rows, 0.0)
            made[v + 1] += jnp.where(lane < off, rows, 0.0)
        else:
            made[v] += rows
    orb_out[0] = jnp.concatenate(made, axis=1).astype(jnp.bfloat16)
    for piece in range(pieces):
        repeat(W - 1, lambda step: green_copy(piece, step).wait_send())
        repeat(W - 1, lambda step: op_copy(piece, step).wait_send())
    repeat(2 * H - 1, lambda step: part_copy(step).wait_send())
    for degree in range(TAYLOR):
        for chunk in range(chunks):
            term_copy(degree, chunk).wait_send()


def per_device(green_blocks, chol_vectors, aux_fields, orbitals, transfer_table):
    C = lax.axis_size("chol")
    H = lax.axis_size("walk")
    KD = green_blocks.shape[2]
    PD = chol_vectors.shape[2]
    N = chol_vectors.shape[3]
    K = transfer_table.shape[0]
    W = C * H
    anywhere = pl.BlockSpec(memory_space=pltpu.HBM)
    pieces = KD // HALF * max(1, PD // 256)
    chol_chunks = 4
    term = pltpu.VMEM((K, NORB, LANES), jnp.bfloat16)
    dma = pltpu.SemaphoreType.DMA
    held = pl.BlockSpec(memory_space=pltpu.VMEM)
    return pl.pallas_call(
        functools.partial(kernel, (C, H, KD, PD, N)),
        out_shape=(
            pltpu.VMEM(aux_fields.shape, jnp.float32),
            pltpu.VMEM(orbitals.shape, jnp.bfloat16),
        ),
        in_specs=[anywhere] * 5,
        out_specs=(held, held),
        scratch_shapes=[
            pltpu.VMEM((KD, PD, N), jnp.bfloat16),
            pltpu.VMEM((W, KD, PD), jnp.bfloat16),
            pltpu.VMEM((2 * H, W, N), jnp.float32),
            pltpu.VMEM((W, 1, N), jnp.float32),
            pltpu.VMEM((W, KD, PD), jnp.bfloat16),
            pltpu.VMEM((C, KD, NORB * NORB), jnp.bfloat16),
            pltpu.VMEM((NORB * KD, LANES), jnp.float32),
            pltpu.VMEM((KD, NORB, C * NORB), jnp.bfloat16),
            pltpu.VMEM((KD, NORB * SPOCC), jnp.bfloat16),
            pltpu.VMEM((KD, NORB, LANES), jnp.float32),
            term,
            term,
            term,
            term,
            pltpu.SMEM(transfer_table.shape[::-1], jnp.int32),
            dma((chol_chunks,)),
            dma((3,)),
            dma((pieces,)),
            dma((pieces, W)),
            dma((pieces, W)),
            dma((2 * H,)),
            dma((2 * H,)),
            dma((pieces, W)),
            dma((pieces, W)),
            dma((TAYLOR, 4)),
            dma((TAYLOR, 4)),
        ],
        compiler_params=pltpu.CompilerParams(
            collective_id=0, has_side_effects=True, vmem_limit_bytes=63 * 1024 * 1024
        ),
        name="walker_step",
    )(transfer_table.T, green_blocks, chol_vectors, aux_fields, orbitals)

def solution(mesh):
    placed = (
        P(("groups", "chol", "walk"), None, "kpt", None),
        P("chol", "kpt", "walk", None),
        P("groups", "chol", None),
        P(("groups", "chol", "walk"), "kpt", None),
        P(),
    )
    return jax.shard_map(
        per_device,
        mesh=mesh,
        in_specs=placed,
        out_specs=(P("groups", "chol", None), P(("groups", "chol", "walk"), "kpt", None)),
        check_vma=False,
    )
```

```python
import functools

import jax
import jax.numpy as jnp
from jax import lax
from jax.experimental import pallas as pl
from jax.experimental.pallas import tpu as pltpu
from jax.sharding import PartitionSpec as P

NORB = 32
SPOCC = 24
TAYLOR = 4
LANES = 128
HALF = 16
MESH = pl.DeviceIdType.MESH


bias_scale = 0.5


def repeat(count, body):
    if count <= 16:
        for step in range(count):
            body(step)
    else:
        lax.fori_loop(0, count, lambda step, carry: (body(step), carry)[1], 0)


def kernel(
    sizes,
    table_in,
    green_ref,
    chol_ref,
    aux_ref,
    orb_ref,
    bias_out,
    orb_out,
    chol_v,
    arrived,
    parts,
    aux_v,
    op_send,
    ops,
    relay,
    blocks,
    orb_v,
    total,
    term0,
    term1,
    term2,
    term3,
    table_ref,
    chol_sem,
    small_sem,
    own_sem,
    green_send,
    green_recv,
    part_send,
    part_recv,
    op_sendsem,
    op_recv,
    term_send,
    term_recv,
):
    C, H, KD, PD, N = sizes
    W = C * H
    halves = KD // HALF
    splits = green_send.shape[0] // halves
    pieces = halves * splits
    width = PD // splits
    my_c, my_h, my_k = lax.axis_index("chol"), lax.axis_index("walk"), lax.axis_index("kpt")
    me = my_c * H + my_h
    terms = (term0, term1, term2, term3)
    quads = C // 4
    chol_chunks = chol_sem.shape[0]
    chunk_k = KD // chol_chunks

    top, low = my_c // (C // 2), lax.rem(my_c, C // 2)

    def peer_at(step):
        near = step // (W // 2)
        rest = step % (W // 2) + near
        pc = lax.rem(top + 1 - near, 2) * (C // 2) + lax.rem(low + rest // H, C // 2)
        ph = lax.rem(my_h + rest % H, H)
        return pc, ph, pc * H + ph

    def rows_of(piece):
        return pl.ds(piece // splits * HALF, HALF)

    def slab_of(h, piece):
        start = h * PD + piece % splits * width
        return pl.ds(pl.multiple_of(start, LANES), width)

    def part_of(piece):
        return pl.ds(piece % splits * width, width)

    barrier = pltpu.get_barrier_semaphore()

    def greet(step):
        pc, ph, _ = peer_at(step)
        pl.semaphore_signal(barrier, inc=1, device_id={"chol": pc, "walk": ph}, device_id_type=MESH)

    repeat(W - 1, greet)

    def greet_other(step):
        pl.semaphore_signal(
            barrier, inc=1, device_id={"walk": step, "kpt": 1 - my_k}, device_id_type=MESH
        )

    repeat(H, greet_other)
    orb_copy = pltpu.make_async_copy(orb_ref.at[0], orb_v, small_sem.at[0])
    orb_copy.start()
    aux_copy = pltpu.make_async_copy(aux_ref, aux_v, small_sem.at[1])
    aux_copy.start()
    table_copy = pltpu.make_async_copy(table_in, table_ref, small_sem.at[2])
    table_copy.start()

    def chol_copy(chunk):
        rows = pl.ds(chunk * chunk_k, chunk_k)
        return pltpu.make_async_copy(chol_ref.at[0, rows], chol_v.at[rows], chol_sem.at[chunk])

    def own_green(piece):
        rows = rows_of(piece)
        return pltpu.make_async_copy(
            green_ref.at[0, my_c, rows, slab_of(my_h, piece)],
            arrived.at[piece, me],
            own_sem.at[piece],
        )

    for piece in range(pieces):
        own_green(piece).start()
    for chunk in range(chol_chunks):
        chol_copy(chunk).start()
    pl.semaphore_wait(barrier, W - 1 + H)

    def green_copy(piece, step):
        pc, ph, _ = peer_at(step)
        rows = rows_of(piece)
        return pltpu.make_async_remote_copy(
            src_ref=green_ref.at[0, pc, rows, slab_of(ph, piece)],
            dst_ref=arrived.at[piece, me],
            send_sem=green_send.at[piece, step],
            recv_sem=green_recv.at[piece, me],
            device_id={"chol": pc, "walk": ph},
            device_id_type=MESH,
        )

    def green_wait(piece, step):
        pc, ph, peer = peer_at(step)
        landed = arrived.at[piece, peer]
        pltpu.make_async_remote_copy(
            src_ref=landed,
            dst_ref=landed,
            send_sem=green_send.at[piece, step],
            recv_sem=green_recv.at[piece, peer],
            device_id={"chol": pc, "walk": ph},
            device_id_type=MESH,
        ).wait_recv()

    for piece in range(pieces):
        repeat(W - 1, lambda step: green_copy(piece, step).start())

    lane = lax.broadcasted_iota(jnp.int32, (KD, LANES), 1)
    orb_copy.wait()
    for l in range(NORB):
        v, off = divmod(l * SPOCC, LANES)
        shift = (LANES - off) % LANES
        piece = orb_v[:, v * LANES : (v + 1) * LANES].astype(jnp.float32)
        if shift:
            piece = pltpu.roll(piece, shift, 1)
        if off + SPOCC > LANES:
            following = orb_v[:, (v + 1) * LANES : (v + 2) * LANES].astype(jnp.float32)
            piece = jnp.where(lane < LANES - off, piece, pltpu.roll(following, shift, 1))
        relay[l * KD : (l + 1) * KD, :] = jnp.where(lane < SPOCC, piece, 0.0)
    for k in range(KD):
        rows = relay[pl.ds(k, NORB, stride=KD), :]
        total[k] = rows
        term0[my_k * KD + k] = rows.astype(jnp.bfloat16)

    chunks = 2
    per_chunk = KD // chunks

    def term_copy(degree, chunk):
        rows = pl.ds(my_k * KD + chunk * per_chunk, per_chunk)
        return pltpu.make_async_remote_copy(
            src_ref=terms[degree].at[rows],
            dst_ref=terms[degree].at[rows],
            send_sem=term_send.at[degree, chunk],
            recv_sem=term_recv.at[degree, chunk],
            device_id={"kpt": 1 - my_k},
            device_id_type=MESH,
        )

    def term_wait(degree, chunk):
        rows = pl.ds((1 - my_k) * KD + chunk * per_chunk, per_chunk)
        pltpu.make_async_remote_copy(
            src_ref=terms[degree].at[rows],
            dst_ref=terms[degree].at[rows],
            send_sem=term_send.at[degree, chunk],
            recv_sem=term_recv.at[degree, chunk],
            device_id={"kpt": 1 - my_k},
            device_id_type=MESH,
        ).wait_recv()

    for chunk in range(chunks):
        term_copy(0, chunk).start()

    partial = jnp.zeros((W, N), jnp.float32)
    for piece in range(pieces):
        own_green(piece).wait()
        repeat(W - 1, lambda step: green_wait(piece, step))
        half, split = divmod(piece, splits)
        k0, p0 = half * HALF, split * width
        if split == 0:
            for chunk in range(chol_chunks // halves):
                chol_copy(half * (chol_chunks // halves) + chunk).wait()
        for group in range(0, HALF, 8):
            rows = arrived[piece].astype(jnp.float32)
            rows = jnp.swapaxes(rows[:, group : group + 8, :], 0, 1)
            left = jnp.concatenate([rows[k] for k in range(8)], axis=1).astype(jnp.bfloat16)
            right = chol_v[k0 + group : k0 + group + 8, p0 : p0 + width].reshape(8 * width, N)
            partial += jnp.dot(left, right, preferred_element_type=jnp.float32)

    slot = my_h * 2 + my_k
    parts[slot] = partial

    def part_copy(step):
        peer = lax.rem(slot + 1 + step, 2 * H)
        return pltpu.make_async_remote_copy(
            src_ref=parts.at[slot],
            dst_ref=parts.at[slot],
            send_sem=part_send.at[step],
            recv_sem=part_recv.at[slot],
            device_id={"walk": peer // 2, "kpt": lax.rem(peer, 2)},
            device_id_type=MESH,
        )

    def part_wait(step):
        peer = lax.rem(slot + 1 + step, 2 * H)
        pltpu.make_async_remote_copy(
            src_ref=parts.at[peer],
            dst_ref=parts.at[peer],
            send_sem=part_send.at[step],
            recv_sem=part_recv.at[peer],
            device_id={"walk": peer // 2, "kpt": lax.rem(peer, 2)},
            device_id_type=MESH,
        ).wait_recv()

    repeat(2 * H - 1, lambda step: part_copy(step).start())
    aux_copy.wait()
    table_copy.wait()
    fields = aux_v[:, 0, :]
    repeat(2 * H - 1, part_wait)
    bias = parts[0]
    for other in range(1, 2 * H):
        bias += parts[other]
    shifted = (fields - jnp.clip(-bias_scale * bias, -1.0, 1.0)).astype(jnp.bfloat16)

    def op_copy(piece, step):
        pc, ph, peer = peer_at(step)
        rows = rows_of(piece)
        return pltpu.make_async_remote_copy(
            src_ref=op_send.at[piece, peer],
            dst_ref=ops.at[piece, my_c, my_h],
            send_sem=op_sendsem.at[piece, step],
            recv_sem=op_recv.at[piece, me],
            device_id={"chol": pc, "walk": ph},
            device_id_type=MESH,
        )

    def op_wait(piece, step):
        pc, ph, peer = peer_at(step)
        rows = rows_of(piece)
        pltpu.make_async_remote_copy(
            src_ref=op_send.at[piece, peer],
            dst_ref=ops.at[piece, pc, ph],
            send_sem=op_sendsem.at[piece, step],
            recv_sem=op_recv.at[piece, peer],
            device_id={"chol": pc, "walk": ph},
            device_id_type=MESH,
        ).wait_recv()

    def own_op(piece):
        rows = rows_of(piece)
        return pltpu.make_async_copy(
            op_send.at[piece, me],
            ops.at[piece, my_c, my_h],
            own_sem.at[piece],
        )

    for piece in range(pieces):
        half, split = divmod(piece, splits)
        k0, p0 = half * HALF, split * width
        made = []
        for group in range(0, HALF, 8):
            right = chol_v[k0 + group : k0 + group + 8, p0 : p0 + width].reshape(8 * width, N)
            out = lax.dot_general(
                shifted, right, (((1,), (1,)), ((), ())), preferred_element_type=jnp.float32
            )
            stacked = jnp.stack([out[:, k * width : (k + 1) * width] for k in range(8)], axis=0)
            made.append(jnp.swapaxes(stacked, 0, 1))
        op_send[piece] = jnp.concatenate(made, axis=1).astype(jnp.bfloat16)
        repeat(W - 1, lambda step: op_copy(piece, step).start())
        own_op(piece).start()

    bias_out[:, 0, :] = bias

    narrow = lax.broadcasted_iota(jnp.int32, (HALF, LANES), 1) // NORB
    for half in range(halves):
        k0 = half * HALF
        for piece in range(half * splits, (half + 1) * splits):
            own_op(piece).wait()
            repeat(W - 1, lambda step: op_wait(piece, step))
        for quad in range(quads):
            for tile in range(NORB * NORB // LANES):
                h, column = divmod(tile * LANES, PD)
                piece, column = half * splits + column // width, column % width
                given = [
                    ops[piece, 4 * quad + j, h, :, column : column + LANES].astype(jnp.float32)
                    for j in range(4)
                ]
                for inner in range(4):
                    made = None
                    for j in range(4):
                        turn = (j - inner) % 4 * NORB
                        value = pltpu.roll(given[j], turn, 1) if turn else given[j]
                        made = value if made is None else jnp.where(narrow == j, value, made)
                    row = (tile * 4 + inner) * HALF
                    relay[row : row + HALF, :] = made
            for k in range(HALF):
                rows = relay[pl.ds(k, NORB, stride=HALF), :]
                blocks[k0 + k, :, quad * LANES : (quad + 1) * LANES] = rows.astype(jnp.bfloat16)

    for degree in range(1, TAYLOR + 1):
        source = terms[degree - 1]
        for chunk in range(chunks):
            term_wait(degree - 1, chunk)
        for chunk in range(chunks):
            for inner in range(per_chunk):
                k = chunk * per_chunk + inner
                right = jnp.concatenate(
                    [source[table_ref[j, my_k * KD + k]] for j in range(C)], axis=0
                )
                update = jnp.dot(blocks[k], right, preferred_element_type=jnp.float32)
                if degree > 1:
                    update = update * (1.0 / degree)
                total[k] += update
                if degree < TAYLOR:
                    terms[degree][my_k * KD + k] = update.astype(jnp.bfloat16)
            if degree < TAYLOR:
                term_copy(degree, chunk).start()

    made = [jnp.zeros((KD, LANES), jnp.float32) for _ in range(NORB * SPOCC // LANES)]
    flat = total.reshape(KD * NORB, LANES)
    for i in range(NORB):
        v, off = divmod(i * SPOCC, LANES)
        rows = flat[pl.ds(i, KD, stride=NORB), :]
        if off:
            rows = pltpu.roll(rows, off, 1)
        if off + SPOCC > LANES:
            made[v] += jnp.where(lane >= off, rows, 0.0)
            made[v + 1] += jnp.where(lane < off, rows, 0.0)
        else:
            made[v] += rows
    orb_out[0] = jnp.concatenate(made, axis=1).astype(jnp.bfloat16)
    for piece in range(pieces):
        repeat(W - 1, lambda step: green_copy(piece, step).wait_send())
        repeat(W - 1, lambda step: op_copy(piece, step).wait_send())
    repeat(2 * H - 1, lambda step: part_copy(step).wait_send())
    for degree in range(TAYLOR):
        for chunk in range(chunks):
            term_copy(degree, chunk).wait_send()


def per_device(green_blocks, chol_vectors, aux_fields, orbitals, transfer_table):
    C = lax.axis_size("chol")
    H = lax.axis_size("walk")
    KD = green_blocks.shape[2]
    PD = chol_vectors.shape[2]
    N = chol_vectors.shape[3]
    K = transfer_table.shape[0]
    W = C * H
    anywhere = pl.BlockSpec(memory_space=pltpu.HBM)
    pieces = KD // HALF * max(1, PD // 256)
    chol_chunks = 4
    term = pltpu.VMEM((K, NORB, LANES), jnp.bfloat16)
    dma = pltpu.SemaphoreType.DMA
    held = pl.BlockSpec(memory_space=pltpu.VMEM)
    return pl.pallas_call(
        functools.partial(kernel, (C, H, KD, PD, N)),
        out_shape=(
            pltpu.VMEM(aux_fields.shape, jnp.float32),
            pltpu.VMEM(orbitals.shape, jnp.bfloat16),
        ),
        in_specs=[anywhere] * 5,
        out_specs=(held, held),
        scratch_shapes=[
            pltpu.VMEM((KD, PD, N), jnp.bfloat16),
            pltpu.VMEM((pieces, W, HALF, KD * PD // (pieces * HALF)), jnp.bfloat16),
            pltpu.VMEM((2 * H, W, N), jnp.float32),
            pltpu.VMEM((W, 1, N), jnp.float32),
            pltpu.VMEM((pieces, W, HALF, KD * PD // (pieces * HALF)), jnp.bfloat16),
            pltpu.VMEM((pieces, C, H, HALF, KD * PD // (pieces * HALF)), jnp.bfloat16),
            pltpu.VMEM((NORB * KD, LANES), jnp.float32),
            pltpu.VMEM((KD, NORB, C * NORB), jnp.bfloat16),
            pltpu.VMEM((KD, NORB * SPOCC), jnp.bfloat16),
            pltpu.VMEM((KD, NORB, LANES), jnp.float32),
            term,
            term,
            term,
            term,
            pltpu.SMEM(transfer_table.shape[::-1], jnp.int32),
            dma((chol_chunks,)),
            dma((3,)),
            dma((pieces,)),
            dma((pieces, W)),
            dma((pieces, W)),
            dma((2 * H,)),
            dma((2 * H,)),
            dma((pieces, W)),
            dma((pieces, W)),
            dma((TAYLOR, 2)),
            dma((TAYLOR, 2)),
        ],
        compiler_params=pltpu.CompilerParams(
            collective_id=0, has_side_effects=True, vmem_limit_bytes=63 * 1024 * 1024
        ),
        name="walker_step",
    )(transfer_table.T, green_blocks, chol_vectors, aux_fields, orbitals)

def solution(mesh):
    placed = (
        P(("groups", "chol", "walk"), None, "kpt", None),
        P("chol", "kpt", "walk", None),
        P("groups", "chol", None),
        P(("groups", "chol", "walk"), "kpt", None),
        P(),
    )
    return jax.shard_map(
        per_device,
        mesh=mesh,
        in_specs=placed,
        out_specs=(P("groups", "chol", None), P(("groups", "chol", "walk"), "kpt", None)),
        check_vma=False,
    )
```
